32 devices in a mesh: seq: 8 (over z, x), tp: 4 (over y, core).
Axes of the slice: x: 2, y: 2, z: 4, core: 2. Of those that a mesh axis runs over, the one named last changes fastest.
Arguments:
- queries: bfloat16 [2048, 8192], P('seq', 'tp'), may hold values from -6 to 6
- keys: bfloat16 [2048, 8192], P('seq', 'tp'), may hold values from -6 to 6
- values: bfloat16 [2048, 8192], P('seq', 'tp'), may hold values from -6 to 6
- norm_gain: float32 [128], replicated, may hold values from 0.1 to 1.9
- out_weight: bfloat16 [8192, 8192], P(None, 'tp'), may hold values from -0.0625 to 0.0625
Outputs:
- layer_out: bfloat16 [2048, 8192], P('seq', 'tp')
The draws below stay inside these ranges and needn't reach their ends.
All inputs are finite; a program needn't handle non-finite values.
Results may differ from the reference program's by a relative error of at most 0.0058.
Values may be sent and summed in bfloat16 or wider, within the bound.
A program may use at most 128 MiB of HBM per device.

```python
import jax
import jax.numpy as jnp
from jax import lax

D = 8192
HEADS = 64
DH = 128
TOK_DEV = 256
TOKENS = 2048
N_SEQ = 8


def block_levels(rng, shape, cuts, smallest, top_value):
    def one(axis_at, shards_of):
        draws = jax.random.uniform(jax.random.fold_in(jax.random.fold_in(rng, 6), axis_at), (shards_of,), jnp.float32, smallest / len(cuts), top_value / len(cuts))
        return jnp.repeat(jnp.exp(draws), shape[axis_at] // shards_of).reshape((-1,) + (1,) * (len(shape) - axis_at - 1))

    gain = one(*cuts[0])
    for cut in cuts[1:]:
        gain = gain * one(*cut)
    return gain


def gaussian(key, extent, scale, most, shards=(), held_as=jnp.bfloat16):
    values = scale * jax.random.normal(key, extent, jnp.float32)
    if shards:
        values = values * block_levels(key, extent, shards, -0.22, 0.18)
    return jnp.clip(values, -most, most).astype(held_as)


def setup_inputs(seed: int = 0) -> dict:
    key_of = jax.random.split(jax.random.key(seed), 6)
    queries = gaussian(key_of[0], (TOKENS, D), 1.0, 6.0, ((0, 8), (1, 4)))
    keys = gaussian(key_of[1], (TOKENS, D), 1.0, 6.0, ((0, 8), (1, 4)))
    values = gaussian(key_of[2], (TOKENS, D), 1.0, 6.0, ((0, 8), (1, 4)))
    norm_gain = jnp.clip(1.0 + 0.18 * jax.random.normal(key_of[3], (DH,), jnp.float32), 0.1, 1.9)
    out_weight = gaussian(key_of[4], (D, D), D ** -0.5, 0.0625, ((1, 4),))
    return dict(queries=queries, keys=keys, values=values, norm_gain=norm_gain, out_weight=out_weight)


epsilon = 1e-06

def head_output(bundle, norm_gain):
    q_head, k_head, v_head = bundle
    q_float = q_head.astype(jnp.float32)
    k_float = k_head.astype(jnp.float32)
    v_float = v_head.astype(jnp.float32)
    states = jnp.einsum('ctk,ctv->ckv', k_float, v_float)
    running = jnp.cumsum(states, axis=0)
    prefix = jnp.concatenate([jnp.zeros_like(states[:1]), running[:-1]], axis=0)
    prefix_batch = lax.optimization_barrier(prefix.astype(jnp.bfloat16)).astype(jnp.float32)
    carried_state = jnp.einsum('ctk,ckv->ctv', q_float, prefix_batch)
    scores = jnp.einsum('ctk,csk->cts', q_float, k_float)
    row_ids = lax.broadcasted_iota(jnp.int32, (TOK_DEV, TOK_DEV), 0)
    col_ids = lax.broadcasted_iota(jnp.int32, (TOK_DEV, TOK_DEV), 1)
    causal = col_ids <= row_ids
    scores = jnp.where(causal[None], scores, jnp.float32(0.0))
    scores_b = lax.optimization_barrier(scores.astype(jnp.bfloat16)).astype(jnp.float32)
    within = jnp.einsum('cts,csv->ctv', scores_b, v_float)
    attended = carried_state + within
    inverse = lax.rsqrt(lax.optimization_barrier(jnp.mean(attended * attended, axis=-1, keepdims=True)) + epsilon)
    return (attended * inverse * norm_gain).astype(jnp.bfloat16)

def split_heads(array):
    return array.reshape(N_SEQ, TOK_DEV, HEADS, DH).transpose(2, 0, 1, 3)

def reference(queries, keys, values, norm_gain, out_weight):

    def one_head(bundle):
        return head_output(bundle, norm_gain)
    normed = lax.map(one_head, (split_heads(queries), split_heads(keys), split_heads(values)))
    normed = normed.transpose(1, 2, 0, 3).reshape(TOKENS, D)
    return jnp.dot(normed, out_weight, preferred_element_type=jnp.float32).astype(jnp.bfloat16)
```

```python
import functools

import jax
import jax.numpy as jnp
from jax import lax
from jax.experimental import pallas as pl
from jax.experimental.pallas import tpu as pltpu
from jax.sharding import PartitionSpec as P

DH = 128
PACK = 2
INNER = 2
EPSILON = 1e-06
MESH = pl.DeviceIdType.MESH
F32 = jnp.float32
BF16 = jnp.bfloat16


def kernel(
    n_seq, n_tp,
    q_hbm, k_hbm, v_hbm, gain_ref, w_hbm, o_ref,
    q_buf, k_buf, v_buf, w_buf, state, x_out, x_in, z_out, z_in, within, normed, acc,
    qkv_sem, w_sem, x_send, x_recv, z_send, z_recv, sib_send, y_send, fwd_send, n_recv,
):
    n_chunks, rows, width = q_buf.shape
    n_out = n_seq // INNER
    n_y = n_tp // 2
    s = lax.axis_index("seq")
    t = lax.axis_index("tp")
    inner, outer = lax.rem(s, INNER), lax.div(s, INNER)
    core, y = lax.rem(t, 2), lax.div(t, 2)
    partner = s + 1 - 2 * inner
    sibling = t + 1 - 2 * core
    has_before = outer > 0
    has_after = outer < n_out - 1
    ahead = [lax.rem(y + d, n_y) * 2 + core for d in range(1, n_y)]
    behind = [lax.rem(y + n_y - d, n_y) * 2 + core for d in range(1, n_y)]
    behind_sib = [lax.rem(y + n_y - d, n_y) * 2 + 1 - core for d in range(1, n_y)]

    def load(which, g):
        src = (k_hbm, v_hbm, q_hbm)[which]
        dst = (k_buf, v_buf, q_buf)[which]
        cols = pl.ds(pl.multiple_of(g * width, width), width)
        return pltpu.make_async_copy(src.at[:, cols], dst.at[g], qkv_sem.at[which, g])

    def load_w(origin, g):
        at = origin * n_chunks + g
        span = pl.ds(pl.multiple_of(at * width, width), width)
        return pltpu.make_async_copy(w_hbm.at[span, :], w_buf.at[at], w_sem.at[at])

    def remote(src, dst, send, recv, seq_to, tp_to):
        return pltpu.make_async_remote_copy(
            src_ref=src, dst_ref=dst, send_sem=send, recv_sem=recv,
            device_id=(seq_to, tp_to), device_id_type=MESH,
        )

    def copy_x(g):
        return remote(x_out.at[g], x_in.at[g], x_send.at[g], x_recv.at[g], partner, t)

    def copy_z(g):
        after = jnp.minimum(s + INNER, n_seq - 1)
        return remote(z_out.at[g], z_in.at[g], z_send.at[g], z_recv.at[g], after, t)

    def copy_sib(g):
        return remote(normed.at[t, g], normed.at[t, g], sib_send.at[g], n_recv.at[t, g], s, sibling)

    def copy_y(d, g):
        return remote(normed.at[t, g], normed.at[t, g], y_send.at[d, g], n_recv.at[t, g], s, ahead[d])

    def copy_fwd(d, g):
        o = behind[d]
        return remote(normed.at[o, g], normed.at[o, g], fwd_send.at[d, g], n_recv.at[o, g], s, sibling)

    def arrived(o, g):
        return remote(normed.at[o, g], normed.at[o, g], sib_send.at[g], n_recv.at[o, g], s, sibling)

    def start_kv(g, _):
        load(0, g).start()
        load(1, g).start()
        return 0

    lax.fori_loop(0, n_chunks, start_kv, 0)

    barrier = pltpu.get_barrier_semaphore()
    for who in [(partner, t), (s, sibling)] + [(s, b) for b in behind]:
        pl.semaphore_signal(barrier, inc=1, device_id=who, device_id_type=MESH)

    @pl.when(has_before)
    def _():
        pl.semaphore_signal(barrier, inc=1, device_id=(s - INNER, t), device_id_type=MESH)

    def start_q(g, _):
        load(2, g).start()
        return 0

    lax.fori_loop(0, n_chunks, start_q, 0)

    pl.semaphore_wait(barrier, 1 + n_y + jnp.where(has_after, 1, 0))

    def make_state(g, _):
        load(0, g).wait()
        load(1, g).wait()
        for h in range(PACK):
            cols = pl.ds(h * DH, DH)
            own = lax.dot_general(
                k_buf[g, :, cols], v_buf[g, :, cols], (((0,), (0,)), ((), ())),
                preferred_element_type=F32,
            )
            state[g, h] = own
            x_out[g, h] = own.astype(x_out.dtype)
        copy_x(g).start()
        return 0

    lax.fori_loop(0, n_chunks, make_state, 0)

    def wait_q(g, _):
        load(2, g).wait()
        return 0

    def start_w(origins):
        def body(g, _):
            for o in origins:
                load_w(o, g).start()
            return 0

        lax.fori_loop(0, n_chunks, body, 0)

    start_w([t, sibling])
    start_w(behind + behind_sib)

    lax.fori_loop(0, n_chunks, wait_q, 0)
    acc[...] = jnp.zeros_like(acc)
    def make_within(g):
        row_ids = lax.broadcasted_iota(jnp.int32, (rows, rows), 0)
        col_ids = lax.broadcasted_iota(jnp.int32, (rows, rows), 1)
        causal = col_ids <= row_ids
        for h in range(PACK):
            cols = pl.ds(h * DH, DH)
            scores = lax.dot_general(
                q_buf[g, :, cols], k_buf[g, :, cols], (((1,), (1,)), ((), ())),
                preferred_element_type=F32,
            )
            scores = jnp.where(causal, scores, 0.0).astype(BF16)
            within[g, :, cols] = jnp.dot(scores, v_buf[g, :, cols], preferred_element_type=F32)

    n_cols = acc.shape[1]
    tile = min(512, n_cols)

    def project(pieces):
        for o, g in pieces:
            load_w(o, g).wait()
        for at in range(0, n_cols, tile):
            cols = pl.ds(at, tile)
            total = acc[:, cols]
            for o, g in pieces:
                total += jnp.dot(
                    normed[o, g], w_buf[o * n_chunks + g, :, cols], preferred_element_type=F32
                )
            acc[:, cols] = total

    make_within(0)

    def step(g, _):
        copy_x(g).wait_recv()

        @pl.when(has_before)
        def _():
            copy_z(g).wait_recv()

        later = inner > 0
        for h in range(PACK):
            other = x_in[g, h].astype(F32)
            before = jnp.where(has_before, z_in[g, h].astype(F32), 0.0)
            z_out[g, h] = (before + (state[g, h] + other)).astype(z_out.dtype)
            state[g, h] = before + jnp.where(later, other, 0.0)

        @pl.when(has_after)
        def _():
            copy_z(g).start()

        for h in range(PACK):
            cols = pl.ds(h * DH, DH)
            prefix = state[g, h].astype(BF16)
            attended = within[g, :, cols] + jnp.dot(
                q_buf[g, :, cols], prefix, preferred_element_type=F32
            )
            inverse = lax.rsqrt(jnp.mean(attended * attended, axis=-1, keepdims=True) + EPSILON)
            normed[t, g, :, cols] = (attended * inverse * gain_ref[...]).astype(BF16)
        for d in range(n_y - 1):
            copy_y(d, g).start()
        copy_sib(g).start()

        make_within(jnp.minimum(g + 1, n_chunks - 1))

        @pl.when(g > 0)
        def _():
            arrived(sibling, g - 1).wait_recv()
            project([(t, g - 1), (sibling, g - 1)])

        return 0

    lax.fori_loop(0, n_chunks, step, 0)
    last = n_chunks - 1
    arrived(sibling, last).wait_recv()
    project([(t, last), (sibling, last)])

    def collect(g, _):
        for d in range(n_y - 1):
            arrived(behind[d], g).wait_recv()
            copy_fwd(d, g).start()

        @pl.when(g > 0)
        def _():
            for d in range(n_y - 1):
                arrived(behind_sib[d], g - 1).wait_recv()
                project([(behind[d], g - 1), (behind_sib[d], g - 1)])

        return 0

    lax.fori_loop(0, n_chunks, collect, 0)
    for d in range(n_y - 1):
        project([(behind[d], last)])
        arrived(behind_sib[d], last).wait_recv()
        project([(behind_sib[d], last)])
    o_ref[...] = acc[...].astype(o_ref.dtype)

    def drain(g, _):
        copy_x(g).wait_send()

        @pl.when(has_after)
        def _():
            copy_z(g).wait_send()

        copy_sib(g).wait_send()
        for d in range(n_y - 1):
            copy_y(d, g).wait_send()
            copy_fwd(d, g).wait_send()
        return 0

    lax.fori_loop(0, n_chunks, drain, 0)


def on_device(n_seq, n_tp, queries, keys, values, norm_gain, out_weight):
    rows, own = queries.shape
    depth, n_cols = out_weight.shape
    width = PACK * DH
    n_chunks = own // width
    n_y = n_tp // 2
    link = BF16 if n_seq // INNER <= 4 else F32
    chunk = (n_chunks, rows, width)
    states = (n_chunks, PACK, DH, DH)
    vmem = pl.BlockSpec(memory_space=pltpu.VMEM)
    hbm = pl.BlockSpec(memory_space=pltpu.HBM)
    dma = pltpu.SemaphoreType.DMA
    flops = 2 * rows * depth * n_cols + 2 * rows * own * (2 * rows + 2 * DH)
    return pl.pallas_call(
        functools.partial(kernel, n_seq, n_tp),
        out_shape=jax.ShapeDtypeStruct((rows, n_cols), BF16),
        in_specs=[hbm, hbm, hbm, vmem, hbm],
        out_specs=vmem,
        scratch_shapes=[
            pltpu.VMEM(chunk, BF16),
            pltpu.VMEM(chunk, BF16),
            pltpu.VMEM(chunk, BF16),
            pltpu.VMEM((depth // width, width, n_cols), BF16),
            pltpu.VMEM(states, F32),
            pltpu.VMEM(states, link),
            pltpu.VMEM(states, link),
            pltpu.VMEM(states, link),
            pltpu.VMEM(states, link),
            pltpu.VMEM(chunk, F32),
            pltpu.VMEM((n_tp,) + chunk, BF16),
            pltpu.VMEM((rows, n_cols), F32),
            dma((3, n_chunks)),
            dma((depth // width,)),
            dma((n_chunks,)),
            dma((n_chunks,)),
            dma((n_chunks,)),
            dma((n_chunks,)),
            dma((n_chunks,)),
            dma((n_y - 1, n_chunks)),
            dma((n_y - 1, n_chunks)),
            dma((n_tp, n_chunks)),
        ],
        compiler_params=pltpu.CompilerParams(
            collective_id=0, has_side_effects=True, vmem_limit_bytes=60 * 1024 * 1024
        ),
        cost_estimate=pl.CostEstimate(
            flops=flops, bytes_accessed=2 * (depth * n_cols + 4 * rows * own), transcendentals=0
        ),
    )(queries, keys, values, norm_gain.reshape(1, DH), out_weight)


def solution(mesh):
    n_seq, n_tp = mesh.shape["seq"], mesh.shape["tp"]
    return jax.shard_map(
        functools.partial(on_device, n_seq, n_tp),
        mesh=mesh,
        in_specs=(P("seq", "tp"), P("seq", "tp"), P("seq", "tp"), P(), P(None, "tp")),
        out_specs=P("seq", "tp"),
        check_vma=False,
    )
```

```python
import functools

import jax
import jax.numpy as jnp
from jax import lax
from jax.experimental import pallas as pl
from jax.experimental.pallas import tpu as pltpu
from jax.sharding import PartitionSpec as P

DH = 128
PACK = 2
INNER = 2
EPSILON = 1e-06
MESH = pl.DeviceIdType.MESH
F32 = jnp.float32
BF16 = jnp.bfloat16


def kernel(
    n_seq, n_tp,
    q_hbm, k_hbm, v_hbm, gain_ref, w_hbm, o_ref,
    q_buf, k_buf, v_buf, w_buf, state, x_out, x_in, z_out, z_in, within, normed, acc,
    qkv_sem, w_sem, x_send, x_recv, z_send, z_recv, sib_send, y_send, fwd_send, n_recv,
):
    n_chunks, rows, width = q_buf.shape
    n_out = n_seq // INNER
    n_y = n_tp // 2
    s = lax.axis_index("seq")
    t = lax.axis_index("tp")
    inner, outer = lax.rem(s, INNER), lax.div(s, INNER)
    core, y = lax.rem(t, 2), lax.div(t, 2)
    partner = s + 1 - 2 * inner
    sibling = t + 1 - 2 * core
    has_before = outer > 0
    has_after = outer < n_out - 1
    ahead = [lax.rem(y + d, n_y) * 2 + core for d in range(1, n_y)]
    behind = [lax.rem(y + n_y - d, n_y) * 2 + core for d in range(1, n_y)]
    behind_sib = [lax.rem(y + n_y - d, n_y) * 2 + 1 - core for d in range(1, n_y)]

    def load(which, g):
        src = (k_hbm, v_hbm, q_hbm)[which]
        dst = (k_buf, v_buf, q_buf)[which]
        cols = pl.ds(pl.multiple_of(g * width, width), width)
        return pltpu.make_async_copy(src.at[:, cols], dst.at[g], qkv_sem.at[which, g])

    def load_w(origin, g):
        at = origin * n_chunks + g
        span = pl.ds(pl.multiple_of(at * width, width), width)
        return pltpu.make_async_copy(w_hbm.at[span, :], w_buf.at[at], w_sem.at[at])

    def remote(src, dst, send, recv, seq_to, tp_to):
        return pltpu.make_async_remote_copy(
            src_ref=src, dst_ref=dst, send_sem=send, recv_sem=recv,
            device_id=(seq_to, tp_to), device_id_type=MESH,
        )

    def copy_x(g):
        return remote(x_out.at[g], x_in.at[g], x_send.at[g], x_recv.at[g], partner, t)

    def copy_z(g):
        after = jnp.minimum(s + INNER, n_seq - 1)
        return remote(z_out.at[g], z_in.at[g], z_send.at[g], z_recv.at[g], after, t)

    def copy_sib(g):
        return remote(normed.at[t, g], normed.at[t, g], sib_send.at[g], n_recv.at[t, g], s, sibling)

    def copy_y(d, g):
        return remote(normed.at[t, g], normed.at[t, g], y_send.at[d, g], n_recv.at[t, g], s, ahead[d])

    def copy_fwd(d, g):
        o = behind[d]
        return remote(normed.at[o, g], normed.at[o, g], fwd_send.at[d, g], n_recv.at[o, g], s, sibling)

    def arrived(o, g):
        return remote(normed.at[o, g], normed.at[o, g], sib_send.at[g], n_recv.at[o, g], s, sibling)

    def start_kv(g, _):
        load(0, g).start()
        load(1, g).start()
        return 0

    lax.fori_loop(0, n_chunks, start_kv, 0)

    barrier = pltpu.get_barrier_semaphore()
    for who in [(partner, t), (s, sibling)] + [(s, b) for b in behind]:
        pl.semaphore_signal(barrier, inc=1, device_id=who, device_id_type=MESH)

    @pl.when(has_before)
    def _():
        pl.semaphore_signal(barrier, inc=1, device_id=(s - INNER, t), device_id_type=MESH)

    def start_q(g, _):
        load(2, g).start()
        return 0

    lax.fori_loop(0, n_chunks, start_q, 0)

    acc[...] = jnp.zeros_like(acc)
    pl.semaphore_wait(barrier, 1 + n_y + jnp.where(has_after, 1, 0))

    def make_state(g, _):
        load(0, g).wait()
        load(1, g).wait()
        for h in range(PACK):
            cols = pl.ds(h * DH, DH)
            own = lax.dot_general(
                k_buf[g, :, cols], v_buf[g, :, cols], (((0,), (0,)), ((), ())),
                preferred_element_type=F32,
            )
            state[g, h] = own
            x_out[g, h] = own.astype(x_out.dtype)
        copy_x(g).start()
        for o in (t, sibling):
            load_w(o, g).start()
        return 0

    lax.fori_loop(0, n_chunks, make_state, 0)

    def wait_q(g, _):
        load(2, g).wait()
        return 0

    lax.fori_loop(0, n_chunks, wait_q, 0)
    def make_within(g):
        row_ids = lax.broadcasted_iota(jnp.int32, (rows, rows), 0)
        col_ids = lax.broadcasted_iota(jnp.int32, (rows, rows), 1)
        causal = col_ids <= row_ids
        for h in range(PACK):
            cols = pl.ds(h * DH, DH)
            scores = lax.dot_general(
                q_buf[g, :, cols], k_buf[g, :, cols], (((1,), (1,)), ((), ())),
                preferred_element_type=F32,
            )
            scores = jnp.where(causal, scores, 0.0).astype(BF16)
            within[g, :, cols] = jnp.dot(scores, v_buf[g, :, cols], preferred_element_type=F32)

    n_cols = acc.shape[1]
    tile = min(512, n_cols)

    def project(pieces):
        for o, g in pieces:
            load_w(o, g).wait()
        for at in range(0, n_cols, tile):
            cols = pl.ds(at, tile)
            total = acc[:, cols]
            for o, g in pieces:
                total += jnp.dot(
                    normed[o, g], w_buf[o * n_chunks + g, :, cols], preferred_element_type=F32
                )
            acc[:, cols] = total

    make_within(0)

    def step(g, _):
        copy_x(g).wait_recv()

        @pl.when(has_before)
        def _():
            copy_z(g).wait_recv()

        later = inner > 0
        for h in range(PACK):
            other = x_in[g, h].astype(F32)
            before = jnp.where(has_before, z_in[g, h].astype(F32), 0.0)
            z_out[g, h] = (before + (state[g, h] + other)).astype(z_out.dtype)
            state[g, h] = before + jnp.where(later, other, 0.0)

        @pl.when(has_after)
        def _():
            copy_z(g).start()

        for h in range(PACK):
            cols = pl.ds(h * DH, DH)
            prefix = state[g, h].astype(BF16)
            attended = within[g, :, cols] + jnp.dot(
                q_buf[g, :, cols], prefix, preferred_element_type=F32
            )
            inverse = lax.rsqrt(jnp.mean(attended * attended, axis=-1, keepdims=True) + EPSILON)
            normed[t, g, :, cols] = (attended * inverse * gain_ref[...]).astype(BF16)
        for d in range(n_y - 1):
            copy_y(d, g).start()
        copy_sib(g).start()
        for o in behind + behind_sib:
            load_w(o, g).start()

        make_within(jnp.minimum(g + 1, n_chunks - 1))

        @pl.when(g > 0)
        def _():
            arrived(sibling, g - 1).wait_recv()
            project([(t, g - 1), (sibling, g - 1)])

        return 0

    lax.fori_loop(0, n_chunks, step, 0)
    last = n_chunks - 1
    arrived(sibling, last).wait_recv()
    project([(t, last), (sibling, last)])

    def collect(g, _):
        for d in range(n_y - 1):
            arrived(behind[d], g).wait_recv()
            copy_fwd(d, g).start()

        @pl.when(g > 0)
        def _():
            for d in range(n_y - 1):
                arrived(behind_sib[d], g - 1).wait_recv()
                project([(behind[d], g - 1), (behind_sib[d], g - 1)])

        return 0

    lax.fori_loop(0, n_chunks, collect, 0)
    for d in range(n_y - 1):
        project([(behind[d], last)])
        arrived(behind_sib[d], last).wait_recv()
        project([(behind_sib[d], last)])
    o_ref[...] = acc[...].astype(o_ref.dtype)

    def drain(g, _):
        copy_x(g).wait_send()

        @pl.when(has_after)
        def _():
            copy_z(g).wait_send()

        copy_sib(g).wait_send()
        for d in range(n_y - 1):
            copy_y(d, g).wait_send()
            copy_fwd(d, g).wait_send()
        return 0

    lax.fori_loop(0, n_chunks, drain, 0)


def on_device(n_seq, n_tp, queries, keys, values, norm_gain, out_weight):
    rows, own = queries.shape
    depth, n_cols = out_weight.shape
    width = PACK * DH
    n_chunks = own // width
    n_y = n_tp // 2
    link = BF16 if n_seq // INNER <= 4 else F32
    chunk = (n_chunks, rows, width)
    states = (n_chunks, PACK, DH, DH)
    vmem = pl.BlockSpec(memory_space=pltpu.VMEM)
    hbm = pl.BlockSpec(memory_space=pltpu.HBM)
    dma = pltpu.SemaphoreType.DMA
    flops = 2 * rows * depth * n_cols + 2 * rows * own * (2 * rows + 2 * DH)
    return pl.pallas_call(
        functools.partial(kernel, n_seq, n_tp),
        out_shape=jax.ShapeDtypeStruct((rows, n_cols), BF16),
        in_specs=[hbm, hbm, hbm, vmem, hbm],
        out_specs=vmem,
        scratch_shapes=[
            pltpu.VMEM(chunk, BF16),
            pltpu.VMEM(chunk, BF16),
            pltpu.VMEM(chunk, BF16),
            pltpu.VMEM((depth // width, width, n_cols), BF16),
            pltpu.VMEM(states, F32),
            pltpu.VMEM(states, link),
            pltpu.VMEM(states, link),
            pltpu.VMEM(states, link),
            pltpu.VMEM(states, link),
            pltpu.VMEM(chunk, F32),
            pltpu.VMEM((n_tp,) + chunk, BF16),
            pltpu.VMEM((rows, n_cols), F32),
            dma((3, n_chunks)),
            dma((depth // width,)),
            dma((n_chunks,)),
            dma((n_chunks,)),
            dma((n_chunks,)),
            dma((n_chunks,)),
            dma((n_chunks,)),
            dma((n_y - 1, n_chunks)),
            dma((n_y - 1, n_chunks)),
            dma((n_tp, n_chunks)),
        ],
        compiler_params=pltpu.CompilerParams(
            collective_id=0, has_side_effects=True, vmem_limit_bytes=60 * 1024 * 1024
        ),
        cost_estimate=pl.CostEstimate(
            flops=flops, bytes_accessed=2 * (depth * n_cols + 4 * rows * own), transcendentals=0
        ),
    )(queries, keys, values, norm_gain.reshape(1, DH), out_weight)


def solution(mesh):
    n_seq, n_tp = mesh.shape["seq"], mesh.shape["tp"]
    return jax.shard_map(
        functools.partial(on_device, n_seq, n_tp),
        mesh=mesh,
        in_specs=(P("seq", "tp"), P("seq", "tp"), P("seq", "tp"), P(), P(None, "tp")),
        out_specs=P("seq", "tp"),
        check_vma=False,
    )
```

```python
import functools

import jax
import jax.numpy as jnp
from jax import lax
from jax.experimental import pallas as pl
from jax.experimental.pallas import tpu as pltpu
from jax.sharding import PartitionSpec as P

DH = 128
PACK = 2
LEAD = 3
INNER = 2
EPSILON = 1e-06
MESH = pl.DeviceIdType.MESH
F32 = jnp.float32
BF16 = jnp.bfloat16


def kernel(
    n_seq, n_tp,
    q_hbm, k_hbm, v_hbm, gain_ref, w_hbm, o_ref,
    q_buf, k_buf, v_buf, w_buf, state, x_out, x_in, z_out, z_in, within, normed, acc,
    qkv_sem, w_sem, x_send, x_recv, z_send, z_recv, sib_send, y_send, fwd_send, n_recv,
):
    n_chunks, rows, width = q_buf.shape
    n_out = n_seq // INNER
    n_y = n_tp // 2
    s = lax.axis_index("seq")
    t = lax.axis_index("tp")
    inner, outer = lax.rem(s, INNER), lax.div(s, INNER)
    core, y = lax.rem(t, 2), lax.div(t, 2)
    partner = s + 1 - 2 * inner
    sibling = t + 1 - 2 * core
    has_before = outer > 0
    has_after = outer < n_out - 1
    ahead = [lax.rem(y + d, n_y) * 2 + core for d in range(1, n_y)]
    behind = [lax.rem(y + n_y - d, n_y) * 2 + core for d in range(1, n_y)]
    behind_sib = [lax.rem(y + n_y - d, n_y) * 2 + 1 - core for d in range(1, n_y)]

    def load(which, g):
        src = (k_hbm, v_hbm, q_hbm)[which]
        dst = (k_buf, v_buf, q_buf)[which]
        cols = pl.ds(pl.multiple_of(g * width, width), width)
        return pltpu.make_async_copy(src.at[:, cols], dst.at[g], qkv_sem.at[which, g])

    def load_w(origin, g):
        at = origin * n_chunks + g
        span = pl.ds(pl.multiple_of(at * width, width), width)
        return pltpu.make_async_copy(w_hbm.at[span, :], w_buf.at[at], w_sem.at[at])

    def remote(src, dst, send, recv, seq_to, tp_to):
        return pltpu.make_async_remote_copy(
            src_ref=src, dst_ref=dst, send_sem=send, recv_sem=recv,
            device_id=(seq_to, tp_to), device_id_type=MESH,
        )

    def copy_x(g):
        return remote(x_out.at[g], x_in.at[g], x_send.at[g], x_recv.at[g], partner, t)

    def copy_z(g):
        after = jnp.minimum(s + INNER, n_seq - 1)
        return remote(z_out.at[g], z_in.at[g], z_send.at[g], z_recv.at[g], after, t)

    def copy_sib(g):
        return remote(normed.at[t, g], normed.at[t, g], sib_send.at[g], n_recv.at[t, g], s, sibling)

    def copy_y(d, g):
        return remote(normed.at[t, g], normed.at[t, g], y_send.at[d, g], n_recv.at[t, g], s, ahead[d])

    def copy_fwd(d, g):
        o = behind[d]
        return remote(normed.at[o, g], normed.at[o, g], fwd_send.at[d, g], n_recv.at[o, g], s, sibling)

    def arrived(o, g):
        return remote(normed.at[o, g], normed.at[o, g], sib_send.at[g], n_recv.at[o, g], s, sibling)

    def start_kv(g, _):
        load(0, g).start()
        load(1, g).start()
        return 0

    lax.fori_loop(0, n_chunks, start_kv, 0)

    barrier = pltpu.get_barrier_semaphore()
    for who in [(partner, t), (s, sibling)] + [(s, b) for b in behind]:
        pl.semaphore_signal(barrier, inc=1, device_id=who, device_id_type=MESH)

    @pl.when(has_before)
    def _():
        pl.semaphore_signal(barrier, inc=1, device_id=(s - INNER, t), device_id_type=MESH)

    def start_q(g, _):
        load(2, g).start()
        return 0

    lax.fori_loop(0, n_chunks, start_q, 0)

    acc[...] = jnp.zeros_like(acc)
    pl.semaphore_wait(barrier, 1 + n_y + jnp.where(has_after, 1, 0))

    def make_state(g, _):
        load(0, g).wait()
        load(1, g).wait()
        for h in range(PACK):
            cols = pl.ds(h * DH, DH)
            own = lax.dot_general(
                k_buf[g, :, cols], v_buf[g, :, cols], (((0,), (0,)), ((), ())),
                preferred_element_type=F32,
            )
            state[g, h] = own
            x_out[g, h] = own.astype(x_out.dtype)
        copy_x(g).start()
        for o in (t, sibling):
            load_w(o, g).start()
        return 0

    lead = min(LEAD, n_chunks)
    lax.fori_loop(0, lead, make_state, 0)

    def wait_q(g, _):
        load(2, g).wait()
        return 0

    lax.fori_loop(0, n_chunks, wait_q, 0)
    def make_within(g):
        row_ids = lax.broadcasted_iota(jnp.int32, (rows, rows), 0)
        col_ids = lax.broadcasted_iota(jnp.int32, (rows, rows), 1)
        causal = col_ids <= row_ids
        for h in range(PACK):
            cols = pl.ds(h * DH, DH)
            scores = lax.dot_general(
                q_buf[g, :, cols], k_buf[g, :, cols], (((1,), (1,)), ((), ())),
                preferred_element_type=F32,
            )
            scores = jnp.where(causal, scores, 0.0).astype(BF16)
            within[g, :, cols] = jnp.dot(scores, v_buf[g, :, cols], preferred_element_type=F32)

    n_cols = acc.shape[1]
    tile = min(512, n_cols)

    def project(pieces):
        for o, g in pieces:
            load_w(o, g).wait()
        for at in range(0, n_cols, tile):
            cols = pl.ds(at, tile)
            total = acc[:, cols]
            for o, g in pieces:
                total += jnp.dot(
                    normed[o, g], w_buf[o * n_chunks + g, :, cols], preferred_element_type=F32
                )
            acc[:, cols] = total

    make_within(0)

    def step(g, _):
        copy_x(g).wait_recv()

        @pl.when(has_before)
        def _():
            copy_z(g).wait_recv()

        later = inner > 0
        for h in range(PACK):
            other = x_in[g, h].astype(F32)
            before = jnp.where(has_before, z_in[g, h].astype(F32), 0.0)
            z_out[g, h] = (before + (state[g, h] + other)).astype(z_out.dtype)
            state[g, h] = before + jnp.where(later, other, 0.0)

        @pl.when(has_after)
        def _():
            copy_z(g).start()

        for h in range(PACK):
            cols = pl.ds(h * DH, DH)
            prefix = state[g, h].astype(BF16)
            attended = within[g, :, cols] + jnp.dot(
                q_buf[g, :, cols], prefix, preferred_element_type=F32
            )
            inverse = lax.rsqrt(jnp.mean(attended * attended, axis=-1, keepdims=True) + EPSILON)
            normed[t, g, :, cols] = (attended * inverse * gain_ref[...]).astype(BF16)
        for d in range(n_y - 1):
            copy_y(d, g).start()
        copy_sib(g).start()
        for o in behind + behind_sib:
            load_w(o, g).start()

        make_within(jnp.minimum(g + 1, n_chunks - 1))

        return 0

    def step_and_state(g, _):
        step(g, 0)
        make_state(g + lead, 0)
        return 0

    lax.fori_loop(0, n_chunks - lead, step_and_state, 0)
    lax.fori_loop(n_chunks - lead, n_chunks, step, 0)
    last = n_chunks - 1

    def collect(g, _):
        for d in range(n_y - 1):
            arrived(behind[d], g).wait_recv()
            copy_fwd(d, g).start()
        arrived(sibling, g).wait_recv()
        project([(t, g), (sibling, g)])

        @pl.when(g > 0)
        def _():
            for d in range(n_y - 1):
                arrived(behind_sib[d], g - 1).wait_recv()
                project([(behind[d], g - 1), (behind_sib[d], g - 1)])

        return 0

    lax.fori_loop(0, n_chunks, collect, 0)
    for d in range(n_y - 1):
        project([(behind[d], last)])
        arrived(behind_sib[d], last).wait_recv()
        project([(behind_sib[d], last)])
    o_ref[...] = acc[...].astype(o_ref.dtype)

    def drain(g, _):
        copy_x(g).wait_send()

        @pl.when(has_after)
        def _():
            copy_z(g).wait_send()

        copy_sib(g).wait_send()
        for d in range(n_y - 1):
            copy_y(d, g).wait_send()
            copy_fwd(d, g).wait_send()
        return 0

    lax.fori_loop(0, n_chunks, drain, 0)


def on_device(n_seq, n_tp, queries, keys, values, norm_gain, out_weight):
    rows, own = queries.shape
    depth, n_cols = out_weight.shape
    width = PACK * DH
    n_chunks = own // width
    n_y = n_tp // 2
    link = BF16 if n_seq // INNER <= 4 else F32
    chunk = (n_chunks, rows, width)
    states = (n_chunks, PACK, DH, DH)
    vmem = pl.BlockSpec(memory_space=pltpu.VMEM)
    hbm = pl.BlockSpec(memory_space=pltpu.HBM)
    dma = pltpu.SemaphoreType.DMA
    flops = 2 * rows * depth * n_cols + 2 * rows * own * (2 * rows + 2 * DH)
    return pl.pallas_call(
        functools.partial(kernel, n_seq, n_tp),
        out_shape=jax.ShapeDtypeStruct((rows, n_cols), BF16),
        in_specs=[hbm, hbm, hbm, vmem, hbm],
        out_specs=vmem,
        scratch_shapes=[
            pltpu.VMEM(chunk, BF16),
            pltpu.VMEM(chunk, BF16),
            pltpu.VMEM(chunk, BF16),
            pltpu.VMEM((depth // width, width, n_cols), BF16),
            pltpu.VMEM(states, F32),
            pltpu.VMEM(states, link),
            pltpu.VMEM(states, link),
            pltpu.VMEM(states, link),
            pltpu.VMEM(states, link),
            pltpu.VMEM(chunk, F32),
            pltpu.VMEM((n_tp,) + chunk, BF16),
            pltpu.VMEM((rows, n_cols), F32),
            dma((3, n_chunks)),
            dma((depth // width,)),
            dma((n_chunks,)),
            dma((n_chunks,)),
            dma((n_chunks,)),
            dma((n_chunks,)),
            dma((n_chunks,)),
            dma((n_y - 1, n_chunks)),
            dma((n_y - 1, n_chunks)),
            dma((n_tp, n_chunks)),
        ],
        compiler_params=pltpu.CompilerParams(
            collective_id=0, has_side_effects=True, vmem_limit_bytes=60 * 1024 * 1024
        ),
        cost_estimate=pl.CostEstimate(
            flops=flops, bytes_accessed=2 * (depth * n_cols + 4 * rows * own), transcendentals=0
        ),
    )(queries, keys, values, norm_gain.reshape(1, DH), out_weight)


def solution(mesh):
    n_seq, n_tp = mesh.shape["seq"], mesh.shape["tp"]
    return jax.shard_map(
        functools.partial(on_device, n_seq, n_tp),
        mesh=mesh,
        in_specs=(P("seq", "tp"), P("seq", "tp"), P("seq", "tp"), P(), P(None, "tp")),
        out_specs=P("seq", "tp"),
        check_vma=False,
    )
```
